256 devices in a mesh: dp: 16 (over z, core), expert: 16 (over y, x).
Axes of the slice: x: 4, y: 4, z: 8, core: 2. Of those that a mesh axis runs over, the one named last changes fastest.
Arguments:
- tokens: bfloat16 [32768, 1024], P(('dp', 'expert')), may hold values from -6 to 6
- grad_out: bfloat16 [32768, 1024], P(('dp', 'expert')), may hold values from -6 to 6
- routes: int32 [32768, 10], P(('dp', 'expert')), may hold values from 0 to 47, all different within a row; in each aligned block of 128 rows (0 to 127, 128 to 255, ...) at most 32 rows name the same one
- combine: bfloat16 [32768, 10], P(('dp', 'expert')), may hold values from 0.049804688 to 0.29882812
- w_gate: bfloat16 [48, 1024, 512], P('expert'), may hold values from -0.1875 to 0.1875
- w_up: bfloat16 [48, 1024, 512], P('expert'), may hold values from -0.1875 to 0.1875
- w_down: bfloat16 [48, 512, 1024], P('expert'), may hold values from -0.25 to 0.25
Outputs:
- grad_tokens: bfloat16 [32768, 1024], P(('dp', 'expert'))
- grad_gate: bfloat16 [48, 1024, 512], P('expert', 'dp')
- grad_up: bfloat16 [48, 1024, 512], P('expert', 'dp')
- grad_down: bfloat16 [48, 512, 1024], P('expert', 'dp')
The draws below stay inside these ranges and needn't reach their ends.
Inputs may be any that keep to these rules, and one draw needn't show every extreme that they name: `routes`: A token's 10 experts are different. Among the 128 tokens of one device no expert is named more than 32 times, a bound that some block reaches.
All inputs are finite; a program needn't handle non-finite values.
Results may differ from the reference program's by a relative error of at most 0.022.
Values may be sent and summed in bfloat16 or wider, within the bound.
A program may use at most 128 MiB of HBM per device.

```python
import math
import jax
import jax.numpy as jnp
import numpy as np
from jax import lax

D = 1024
FF = 512
TOP = 10
TOK_DEV = 128
EXPERTS = 48
CAP = 32
TOKENS = 32768
N_DP = 16


def shard_levels(own_key, dims, cuts, least, high):
    level = 1.0
    for position, parts in cuts:
        draws = jax.random.uniform(jax.random.fold_in(jax.random.fold_in(own_key, 6), position), (parts,), jnp.float32, least / len(cuts), high / len(cuts))
        level = level * jnp.repeat(jnp.exp(draws), dims[position] // parts).reshape((-1,) + (1,) * (len(dims) - 1 - position))
    return level


def deal_out(own_key, own, number, rows, number_of, top, most, skew):
    ranking = jax.random.permutation(own_key, number_of)
    crowded, usual = shares(number_of, rows * top, most, skew, True), shares(number_of, rows * top, most, skew, False)
    places = jnp.arange(number_of)

    def named(lengths, offset_by):
        used = int((lengths > 0).sum())
        fixed = max(1, used // 4)
        moved = fixed + (places - fixed + offset_by * (used - fixed)) % max(1, number_of - fixed)
        return jnp.zeros((number_of,), jnp.int32).at[ranking[jnp.where(places < fixed, places, moved)]].set(jnp.asarray(lengths, jnp.int32))

    lengths = jnp.where(number % 4 == 0, named(crowded, number // 4), named(usual, number - number // 4 - 1))
    mixed = jax.random.permutation(jax.random.fold_in(own, 3), number_of)
    giver, receiver = mixed[0:number_of // 2 * 2:2], mixed[1:number_of // 2 * 2:2]
    slack = jnp.minimum(lengths[giver] - 1, most - lengths[receiver]) // 2
    slack = jnp.where((giver == ranking[0]) | (receiver == ranking[0]) | (lengths[receiver] == 0), 0, jnp.maximum(slack, 0))
    moved = jax.random.randint(jax.random.fold_in(own, 4), (number_of // 2,), 0, 1 << 20) % (slack + 1)
    lengths = lengths.at[giver].add(-moved).at[receiver].add(moved)
    members = jnp.searchsorted(jnp.cumsum(lengths), jnp.arange(rows * top), side="right").astype(jnp.int32)
    grid = members.reshape(top, rows).T
    grid = grid[jax.random.permutation(jax.random.fold_in(own, 1), rows)]
    offset_by = jax.random.randint(jax.random.fold_in(own, 2), (rows, 1), 0, top)
    return jnp.take_along_axis(grid, (jnp.arange(top)[None, :] + offset_by) % top, axis=1)


def shares(number_of, total, most, slope, full):
    loads = [(1 << 20) // math.isqrt(grade ** slope) + 1 for grade in range(1, number_of + 1)]
    largest = most if full else min(most, max(-(-total // number_of), total * loads[0] // sum(loads)))
    least = 1 if total - largest >= number_of - 1 else 0
    given, rest = [largest] + [least] * (number_of - 1), total - largest - least * (number_of - 1)
    while rest > 0:
        free = [i for i in range(1, number_of) if given[i] < largest] or [i for i in range(1, number_of) if given[i] < most]
        pool, budget = sum([loads[i] for i in free]), rest
        for i in free:
            more = min(most - given[i], max(1, budget * loads[i] // pool), rest)
            given[i] = given[i] + more
            rest = rest - more
    return np.array(given)


def normal_values(own_key, extent, scale, limit, cuts=(), held_as=jnp.bfloat16):
    level = shard_levels(own_key, extent, cuts, -0.22, 0.18) if cuts else 1.0
    result = jax.random.normal(own_key, extent, jnp.float32) * scale * level
    return jnp.minimum(jnp.maximum(result, -limit), limit).astype(held_as)


def setup_inputs(seed: int = 0) -> dict:
    arg_keys = jax.random.split(jax.random.key(seed), 8)
    tokens = normal_values(arg_keys[0], (TOKENS, D), 1.0, 6.0, ((0, 256),))
    grad_out = normal_values(arg_keys[1], (TOKENS, D), 1.0, 6.0, ((0, 256),))
    routes_keys = jax.random.split(jax.random.fold_in(arg_keys[2], 1), TOKENS // TOK_DEV)
    routes_turns = jax.random.permutation(jax.random.fold_in(arg_keys[2], 3), TOKENS // TOK_DEV)
    routes = jax.vmap(lambda own, number: deal_out(jax.random.fold_in(arg_keys[2], 2), own, number, TOK_DEV, EXPERTS, TOP, CAP, 2))(routes_keys, routes_turns).reshape((TOKENS, TOP))
    combine = jnp.clip(0.049804688 + 0.24902344 * jax.random.uniform(arg_keys[3], (TOKENS, TOP), jnp.float32) ** shard_levels(arg_keys[3], (TOKENS, TOP), ((0, 256),), -0.2, 0.2), 0.049804688, 0.29882812).astype(jnp.bfloat16)
    w_gate = normal_values(arg_keys[4], (EXPERTS, D, FF), D ** -0.5, 0.1875, ((0, 16),))
    w_up = normal_values(arg_keys[5], (EXPERTS, D, FF), D ** -0.5, 0.1875, ((0, 16),))
    w_down = normal_values(arg_keys[6], (EXPERTS, FF, D), FF ** -0.5, 0.25, ((0, 16),))
    return dict(tokens=tokens, grad_out=grad_out, routes=routes, combine=combine, w_gate=w_gate, w_up=w_up, w_down=w_down)


def slot_ranks(route_block, expert_total):
    flat_ids = route_block.reshape(-1)
    marks = (flat_ids[:, None] == jnp.arange(expert_total, dtype=jnp.int32)[None, :]).astype(jnp.int32)
    return jnp.sum((jnp.cumsum(marks, axis=0) - 1) * marks, axis=1).astype(jnp.int32)


def build_slots(route_block, expert_total, slot_depth):
    flat_ids = route_block.reshape(-1)
    pair_total = flat_ids.shape[0]
    slot_rank = slot_ranks(route_block, expert_total)
    slots = jnp.full((expert_total, slot_depth), pair_total, dtype=jnp.int32)
    slots = slots.at[flat_ids, slot_rank].set(jnp.arange(pair_total, dtype=jnp.int32))
    return slots, slot_rank


def contract_last(left, right):
    return lax.dot_general(left, right, (((1,), (1,)), ((), ())), preferred_element_type=jnp.float32)


def contract_first(left, right):
    return lax.dot_general(left, right, (((0,), (0,)), ((), ())), preferred_element_type=jnp.float32)


def group_sum(left, right):
    def add_group(total, pieces):
        partial_term = contract_first(pieces[0], pieces[1]).astype(jnp.bfloat16)
        partial_term = lax.optimization_barrier(partial_term)
        return total + partial_term.astype(jnp.float32), None

    start = jnp.zeros((left.shape[2], right.shape[2]), jnp.float32)
    total, unused = lax.scan(add_group, start, (left, right))
    return total.astype(jnp.bfloat16)


def expert_backward(rows_x, rows_dy, rows_c, gate_w, up_w, down_w):
    gate_pre = jnp.dot(rows_x, gate_w, preferred_element_type=jnp.float32)
    up_pre = jnp.dot(rows_x, up_w, preferred_element_type=jnp.float32)
    sigmoid_gate = jax.nn.sigmoid(gate_pre)
    hidden = (gate_pre * sigmoid_gate * up_pre).astype(jnp.bfloat16)
    d_out = (rows_c[:, None] * rows_dy.astype(jnp.float32)).astype(jnp.bfloat16)
    d_hidden = contract_last(d_out, down_w)
    d_gate = (d_hidden * up_pre * sigmoid_gate * (1.0 + gate_pre * (1.0 - sigmoid_gate))).astype(jnp.bfloat16)
    d_up = (d_hidden * gate_pre * sigmoid_gate).astype(jnp.bfloat16)
    d_rows = (contract_last(d_gate, gate_w) + contract_last(d_up, up_w)).astype(jnp.bfloat16)
    return hidden, d_out, d_gate, d_up, d_rows


def reference(tokens, grad_out, routes, combine, w_gate, w_up, w_down):
    sources = TOKENS // TOK_DEV
    pair_total = TOK_DEV * TOP
    blocks = routes.reshape(sources, TOK_DEV, TOP)
    slots, slot_rank = jax.vmap(lambda route_block: build_slots(route_block, EXPERTS, CAP))(blocks)
    filled = slots < pair_total
    pair_base = (jnp.arange(sources, dtype=jnp.int32) * pair_total)[:, None, None]
    global_pair = jnp.where(filled, slots + pair_base, 0).astype(jnp.int32)
    weight_flat = combine.reshape(-1).astype(jnp.float32)

    def one_expert(grad_accum, expert_index):
        is_live = filled[:, expert_index, :].reshape(-1)
        pair_index = global_pair[:, expert_index, :].reshape(-1)
        token_index = (pair_index // TOP).astype(jnp.int32)
        rows_x = jnp.where(is_live[:, None], tokens[token_index], jnp.zeros((), jnp.bfloat16))
        rows_dy = jnp.where(is_live[:, None], grad_out[token_index], jnp.zeros((), jnp.bfloat16))
        rows_c = jnp.where(is_live, weight_flat[pair_index], jnp.zeros((), jnp.float32))
        hidden, d_out, d_gate, d_up, d_rows = expert_backward(
            rows_x, rows_dy, rows_c, w_gate[expert_index], w_up[expert_index], w_down[expert_index])
        added = jnp.where(is_live[:, None], d_rows.astype(jnp.float32), jnp.zeros((), jnp.float32))
        grad_accum = grad_accum.at[token_index].add(added)
        x_groups = rows_x.reshape(N_DP, -1, D)
        grad_g = group_sum(x_groups, d_gate.reshape(N_DP, -1, FF))
        grad_u = group_sum(x_groups, d_up.reshape(N_DP, -1, FF))
        grad_d = group_sum(hidden.reshape(N_DP, -1, FF), d_out.reshape(N_DP, -1, D))
        return grad_accum, (grad_g, grad_u, grad_d)

    start_accum = jnp.zeros((TOKENS, D), jnp.float32)
    totals, grads = lax.scan(one_expert, start_accum, jnp.arange(EXPERTS, dtype=jnp.int32))
    return totals.astype(jnp.bfloat16), grads[0], grads[1], grads[2]
```

```python
import functools

import jax
import jax.numpy as jnp
from jax import lax
from jax.experimental import pallas as pl
from jax.experimental.pallas import tpu as pltpu
from jax.sharding import PartitionSpec as P

MESH = pl.DeviceIdType.MESH
BF = jnp.bfloat16
F32 = jnp.float32
SIDE = 4
BATCHES = (
    ((0, 0), (1, 0), (3, 0), (0, 1)),
    ((0, 3), (1, 1), (1, 3), (3, 1)),
    ((3, 3), (2, 0), (0, 2), (2, 1)),
    ((2, 3), (1, 2), (3, 2), (2, 2)),
)


def dot_nn(a, b):
    return lax.dot_general(a, b, (((1,), (0,)), ((), ())), preferred_element_type=F32)


def dot_nt(a, b):
    return lax.dot_general(a, b, (((1,), (1,)), ((), ())), preferred_element_type=F32)


def dot_tn(a, b):
    return lax.dot_general(a, b, (((0,), (0,)), ((), ())), preferred_element_type=F32)


def kernel(
    dims,
    tok_ref, gout_ref, routes_ref, comb_ref, wg_ref, wu_ref, wd_ref,
    gt_out, gg_out, gu_out, gd_out,
    gx, gy, gc, wg, wu, wd, xr, do, hid, dgu, drows, pm,
    t0, t1, ra0, ra1, rb0, rb1, sa0, sa1, sb0, sb1,
    wp, sib, rz,
    local_sem, send_sem, recv_sem,
):
    tok, width, ff, held, cap, top, nz = dims
    half = tok // 2
    hw = width // 2
    rows_b = 4 * cap
    dp = lax.axis_index("dp")
    ex = lax.axis_index("expert")
    core, z = lax.rem(dp, 2), lax.div(dp, 2)
    px, py = lax.rem(ex, SIDE), lax.div(ex, SIDE)

    def near(axis, step):
        if axis == "x":
            return (dp, py * SIDE + lax.rem(px + step + SIDE, SIDE))
        if axis == "y":
            return (dp, lax.rem(py + step + SIDE, SIDE) * SIDE + px)
        if axis == "z":
            return (lax.rem(z + step + nz, nz) * 2 + core, ex)
        return (z * 2 + 1 - core, ex)

    partners = [near("x", 1), near("x", -1), near("y", 1), near("y", -1),
                near("z", 1), near("z", -1), near("core", 1)]

    count = [0]
    sent = []

    def push(src, dst, where):
        k = count[0]
        count[0] += 1
        copy = pltpu.make_async_remote_copy(
            src_ref=src, dst_ref=dst, send_sem=send_sem.at[k], recv_sem=recv_sem.at[k],
            device_id=where, device_id_type=MESH,
        )
        copy.start()
        sent.append(copy)
        return copy

    own_x = pltpu.make_async_copy(tok_ref, gx.at[0], local_sem.at[0])
    own_y = pltpu.make_async_copy(gout_ref, gy.at[0], local_sem.at[1])
    own_x.start()
    own_y.start()
    loads = [pltpu.make_async_copy(a, b, local_sem.at[2 + i])
             for i, (a, b) in enumerate(((wg_ref, wg), (wu_ref, wu), (wd_ref, wd)))]

    barrier = pltpu.get_barrier_semaphore()
    for who in partners:
        pl.semaphore_signal(barrier, inc=1, device_id=who, device_id_type=MESH)

    peers = SIDE * SIDE
    ids = lax.broadcasted_iota(jnp.int32, (peers, tok), 0) * held
    for j in range(held):
        total = jnp.zeros((peers, tok), F32)
        for k in range(top):
            total = total + jnp.where(
                routes_ref[k:k + 1, :] == ids + j, comb_ref[k:k + 1, :].astype(F32), 0.0)
        gc[0, :, j * tok:(j + 1) * tok] = total.astype(BF)

    own_x.wait()
    own_y.wait()
    pl.semaphore_wait(barrier, len(partners))

    arrays = {"c": (gc, "x", "y"), "x": (gx, "x", "y"), "y": (gy, "y", "x")}
    coming = {}

    def slot(name, o1, o2):
        return o2 * SIDE + o1 if arrays[name][1] == "x" else o1 * SIDE + o2

    def hop(name, o1, o2, which, step, part=None):
        ref, axis = arrays[name][0], arrays[name][which]
        if which == 1:
            l1, l2 = (o1 - step) % SIDE, o2
        else:
            l1, l2 = o1, (o2 - step) % SIDE
        src, dst = ref.at[slot(name, o1, o2)], ref.at[slot(name, l1, l2)]
        if part is not None:
            src, dst = src.at[pl.ds(part * half, half)], dst.at[pl.ds(part * half, half)]
        coming.setdefault((name, l1, l2), []).append(push(src, dst, near(axis, step)))

    def onward(name, o1, o2, which, off):
        if name == "c":
            if off == 3:
                hop(name, o1, o2, which, 1)
        else:
            hop(name, o1, o2, which, 1 if off == 3 else -1, 0 if off == 3 else 1)

    def arrive(name, o1, o2):
        for copy in coming[(name, o1, o2)]:
            copy.wait_recv()
        if o2 == 0:
            if o1 in (1, 3):
                onward(name, o1, o2, 1, o1)
            for step in (1, -1):
                hop(name, o1, o2, 2, step)
        elif o2 in (1, 3):
            onward(name, o1, o2, 2, o2)

    for which in (1, 2):
        for name in ("c", "x", "y"):
            for step in (1, -1):
                hop(name, 0, 0, which, step)
    for load in loads:
        load.start()

    def arrivals(*offsets):
        for o1, o2 in offsets:
            for name in ("c", "x", "y"):
                arrive(name, o1, o2)

    lower = lax.broadcasted_iota(jnp.int32, (tok, tok), 0)
    upper = lax.broadcasted_iota(jnp.int32, (tok, tok), 1)
    before = (lower < upper).astype(BF)
    slots_in = lax.broadcasted_iota(jnp.int32, (cap, tok), 0).astype(F32)
    mine = lax.broadcasted_iota(jnp.int32, (peers, held * tok), 0) == ex

    def select(i, ox, oy):
        s = oy * SIDE + ox
        weight = jnp.sum(jnp.where(mine, gc[s].astype(F32), 0.0), axis=0, keepdims=True)
        named = jnp.where(weight > 0.0, 1.0, 0.0)
        picks = []
        for j in range(held):
            lane = named[:, j * tok:(j + 1) * tok]
            rank = dot_nn(jnp.broadcast_to(lane, (16, tok)).astype(BF), before)[0:1, :]
            picks.append(jnp.where((slots_in == rank) & (lane > 0.0), 1.0, 0.0))
        pick = jnp.concatenate(picks, axis=0)
        scaled = jnp.concatenate(
            [picks[j] * weight[:, j * tok:(j + 1) * tok] for j in range(held)], axis=0).astype(BF)
        pick = pick.astype(BF)
        pm[i % 4] = pick
        rows_x = dot_nn(pick, gx[s]).astype(BF)
        rows_d = dot_nn(scaled, gy[s]).astype(BF)
        for j in range(held):
            xr[j, i * cap:(i + 1) * cap, :] = rows_x[j * cap:(j + 1) * cap]
            do[j, i * cap:(i + 1) * cap, :] = rows_d[j * cap:(j + 1) * cap]

    def batch(b):
        sources = BATCHES[b]
        for i, (ox, oy) in enumerate(sources):
            select(4 * b + i, ox, oy)
        rows = slice(b * rows_b, (b + 1) * rows_b)

        def expert(e, carry):
            x, d = xr[e, rows, :], do[e, rows, :]
            gate = dot_nn(x, wg[e])
            up = dot_nn(x, wu[e])
            sg = jax.nn.sigmoid(gate)
            hid[e, rows, :] = (gate * sg * up).astype(BF)
            dh = dot_nt(d, wd[e])
            dgate = (dh * up * sg * (1.0 + gate * (1.0 - sg))).astype(BF)
            dup = (dh * gate * sg).astype(BF)
            dgu[e, rows, 0:ff] = dgate
            dgu[e, rows, ff:2 * ff] = dup
            back = (dot_nt(dgate, wg[e]) + dot_nt(dup, wu[e])).astype(BF)
            for i in range(4):
                drows[i, e] = back[i * cap:(i + 1) * cap]
            return carry

        lax.fori_loop(0, held, expert, 0)
        for i, (ox, oy) in enumerate(sources):
            part = dot_tn(pm[i], drows[i].reshape(held * cap, width)).astype(BF)
            t0[ox, oy] = part[:, 0:hw]
            t1[oy, ox] = part[:, hw:width]

    arrivals((1, 0), (3, 0))
    arrivals((0, 1), (0, 3))
    arrivals((2, 0))
    for load in loads:
        load.wait()
    batch(0)
    arrivals((1, 1), (1, 3), (3, 1), (3, 3))
    batch(1)
    arrivals((0, 2), (2, 1), (2, 3))
    arrivals((1, 2))
    batch(2)
    arrivals((3, 2), (2, 2))
    batch(3)

    def far_send(t, ra, axis):
        return [push(t.at[2, :, pl.ds(0, half)], ra.at[0], near(axis, 1)),
                push(t.at[2, :, pl.ds(half, half)], ra.at[1], near(axis, -1))]

    def near_send(t, ra, rb, axis, copies):
        copies[0].wait_recv()
        copies[1].wait_recv()
        for i in range(SIDE):
            t[1, i, 0:half] = (t[1, i, 0:half].astype(F32) + ra[0, i].astype(F32)).astype(BF)
            t[3, i, half:tok] = (t[3, i, half:tok].astype(F32) + ra[1, i].astype(F32)).astype(BF)
        return [push(t.at[1], rb.at[0], near(axis, 1)), push(t.at[3], rb.at[1], near(axis, -1))]

    def near_sum(t, rb, copies):
        copies[0].wait_recv()
        copies[1].wait_recv()
        for i in range(SIDE):
            t[0, i] = (t[0, i].astype(F32) + rb[0, i].astype(F32) + rb[1, i].astype(F32)).astype(BF)

    def far_send2(t, sa, axis):
        return [push(t.at[0, 2, pl.ds(0, half)], sa.at[0], near(axis, 1)),
                push(t.at[0, 2, pl.ds(half, half)], sa.at[1], near(axis, -1))]

    def near_send2(t, sa, sb, axis, copies):
        copies[0].wait_recv()
        copies[1].wait_recv()
        t[0, 1, 0:half] = (t[0, 1, 0:half].astype(F32) + sa[0].astype(F32)).astype(BF)
        t[0, 3, half:tok] = (t[0, 3, half:tok].astype(F32) + sa[1].astype(F32)).astype(BF)
        return [push(t.at[0, 1], sb.at[0], near(axis, 1)), push(t.at[0, 3], sb.at[1], near(axis, -1))]

    def last_sum(t, sb, at, copies):
        copies[0].wait_recv()
        copies[1].wait_recv()
        gt_out[:, at:at + hw] = (
            t[0, 0].astype(F32) + sb[0].astype(F32) + sb[1].astype(F32)).astype(BF)

    gr, dr = width // (2 * nz), ff // (2 * nz)

    def weights(e):
        def piece(p, carry):
            at = pl.multiple_of(p * 4 * gr, 4 * gr)
            res = dot_tn(xr[e, :, pl.ds(at, 4 * gr)], dgu[e]).astype(BF)
            for zz in range(2):
                for c in range(2):
                    for d in range(2):
                        wp[e, c, d, 2 * p + zz, 0:gr, :] = res[
                            (2 * zz + c) * gr:(2 * zz + c + 1) * gr, d * ff:(d + 1) * ff]
            at = pl.multiple_of(p * 4 * dr, 4 * dr)
            res = dot_tn(hid[e, :, pl.ds(at, 4 * dr)], do[e]).astype(BF)
            for zz in range(2):
                for c in range(2):
                    for d in range(2):
                        wp[e, c, d, 2 * p + zz, gr:gr + dr, :] = res[
                            (2 * zz + c) * dr:(2 * zz + c + 1) * dr, d * hw:(d + 1) * hw]
            return carry

        lax.fori_loop(0, nz // 2, piece, 0)
        return push(wp.at[e, 1 - core], sib.at[e], near("core", 1))

    ring = {}

    def ring_step(e, d, k):
        b = lax.rem(z - 1 - k + 2 * nz, nz) if d == 0 else lax.rem(z + 1 + k, nz)
        total = wp[e, core, d, b].astype(F32) + sib[e, d, b].astype(F32)
        if k > 0:
            ring[(e, d)].wait_recv()
            total = total + rz[e, d, k - 1].astype(F32)
        total = total.astype(BF)
        if k < nz - 1:
            wp[e, core, d, b] = total
            ring[(e, d)] = push(
                wp.at[e, core, d, b], rz.at[e, d, k], near("z", 1 if d == 0 else -1))
        else:
            out = gg_out if d == 0 else gu_out
            out[e] = total[0:gr]
            gd_out[e, :, d * hw:(d + 1) * hw] = total[gr:gr + dr]

    ca0, ca1 = far_send(t0, ra0, "x"), far_send(t1, ra1, "y")
    pair = [weights(0)]
    pair.append(weights(1))
    pair[0].wait_recv()
    ring_step(0, 0, 0)
    ring_step(0, 1, 0)
    cb0 = near_send(t0, ra0, rb0, "x", ca0)
    cb1 = near_send(t1, ra1, rb1, "y", ca1)
    pair.append(weights(2))
    for e in (1, 2):
        pair[e].wait_recv()
        ring_step(e, 0, 0)
        ring_step(e, 1, 0)
    for k in range(1, nz):
        for e in range(held):
            for d in range(2):
                ring_step(e, d, k)
        if k == 1:
            near_sum(t0, rb0, cb0)
            ca0 = far_send2(t0, sa0, "y")
            near_sum(t1, rb1, cb1)
            ca1 = far_send2(t1, sa1, "x")
        if k == 2:
            cb0 = near_send2(t0, sa0, sb0, "y", ca0)
            cb1 = near_send2(t1, sa1, sb1, "x", ca1)
        if k == 3:
            last_sum(t0, sb0, 0, cb0)
            last_sum(t1, sb1, hw, cb1)
    for copy in sent:
        copy.wait_send()


COPIES = 15 + 40 + 16 + 3


def shards(tokens, grad_out, routes, combine, w_gate, w_up, w_down):
    tok, width = tokens.shape
    top = routes.shape[1]
    held, unused, ff = w_gate.shape
    peers = lax.axis_size("expert")
    nz = lax.axis_size("dp") // 2
    cap = 8 * ((tok * top * 6 // (5 * peers * held) + 7) // 8)
    dims = (tok, width, ff, held, cap, top, nz)
    rows, hw, half = peers * cap, width // 2, tok // 2
    block = width // (2 * nz) + ff // (2 * nz)
    copies = COPIES + held * 2 * (nz - 1)
    any_spec = pl.BlockSpec(memory_space=pl.ANY)
    vmem_spec = pl.BlockSpec(memory_space=pltpu.VMEM)
    flops = 16 * rows * held * width * ff
    return pl.pallas_call(
        functools.partial(kernel, dims),
        out_shape=(
            jax.ShapeDtypeStruct((tok, width), BF),
            jax.ShapeDtypeStruct((held, width // (2 * nz), ff), BF),
            jax.ShapeDtypeStruct((held, width // (2 * nz), ff), BF),
            jax.ShapeDtypeStruct((held, ff // (2 * nz), width), BF),
        ),
        in_specs=[any_spec, any_spec, vmem_spec, vmem_spec, any_spec, any_spec, any_spec],
        out_specs=(vmem_spec,) * 4,
        scratch_shapes=[
            pltpu.VMEM((peers, tok, width), BF),
            pltpu.VMEM((peers, tok, width), BF),
            pltpu.VMEM((peers, peers, held * tok), BF),
            pltpu.VMEM((held, width, ff), BF),
            pltpu.VMEM((held, width, ff), BF),
            pltpu.VMEM((held, ff, width), BF),
            pltpu.VMEM((held, rows, width), BF),
            pltpu.VMEM((held, rows, width), BF),
            pltpu.VMEM((held, rows, ff), BF),
            pltpu.VMEM((held, rows, 2 * ff), BF),
            pltpu.VMEM((4, held, cap, width), BF),
            pltpu.VMEM((4, held * cap, tok), BF),
            pltpu.VMEM((SIDE, SIDE, tok, hw), BF),
            pltpu.VMEM((SIDE, SIDE, tok, hw), BF),
            pltpu.VMEM((2, SIDE, half, hw), BF),
            pltpu.VMEM((2, SIDE, half, hw), BF),
            pltpu.VMEM((2, SIDE, tok, hw), BF),
            pltpu.VMEM((2, SIDE, tok, hw), BF),
            pltpu.VMEM((2, half, hw), BF),
            pltpu.VMEM((2, half, hw), BF),
            pltpu.VMEM((2, tok, hw), BF),
            pltpu.VMEM((2, tok, hw), BF),
            pltpu.VMEM((held, 2, 2, nz, block, ff), BF),
            pltpu.VMEM((held, 2, nz, block, ff), BF),
            pltpu.VMEM((held, 2, nz - 1, block, ff), BF),
            pltpu.SemaphoreType.DMA((5,)),
            pltpu.SemaphoreType.DMA((copies,)),
            pltpu.SemaphoreType.DMA((copies,)),
        ],
        cost_estimate=pl.CostEstimate(
            flops=flops, bytes_accessed=12 * 1024 * 1024, transcendentals=rows * held * ff),
        compiler_params=pltpu.CompilerParams(
            collective_id=0, has_side_effects=True, vmem_limit_bytes=62 * 1024 * 1024),
    )(tokens, grad_out, routes.T, combine.T, w_gate, w_up, w_down)


def solution(mesh):
    return jax.shard_map(
        shards,
        mesh=mesh,
        in_specs=(
            P(("dp", "expert"), None),
            P(("dp", "expert"), None),
            P(("dp", "expert"), None),
            P(("dp", "expert"), None),
            P("expert", None, None),
            P("expert", None, None),
            P("expert", None, None),
        ),
        out_specs=(
            P(("dp", "expert"), None),
            P("expert", "dp", None),
            P("expert", "dp", None),
            P("expert", "dp", None),
        ),
        check_vma=False,
    )
```

```python
import functools

import jax
import jax.numpy as jnp
from jax import lax
from jax.experimental import pallas as pl
from jax.experimental.pallas import tpu as pltpu
from jax.sharding import PartitionSpec as P

MESH = pl.DeviceIdType.MESH
BF = jnp.bfloat16
F32 = jnp.float32
SIDE = 4
BATCHES = (
    ((0, 0), (3, 0), (1, 0), (0, 3), (0, 1)),
    ((3, 3), (3, 1), (1, 3), (1, 1), (2, 0), (0, 2)),
    ((2, 3), (2, 1), (3, 2), (1, 2), (2, 2)),
)
STARTS = (0, 5, 11, 16)


def dot_nn(a, b):
    return lax.dot_general(a, b, (((1,), (0,)), ((), ())), preferred_element_type=F32)


def dot_nt(a, b):
    return lax.dot_general(a, b, (((1,), (1,)), ((), ())), preferred_element_type=F32)


def dot_tn(a, b):
    return lax.dot_general(a, b, (((0,), (0,)), ((), ())), preferred_element_type=F32)


def kernel(
    dims,
    tok_ref, gout_ref, routes_ref, comb_ref, wg_ref, wu_ref, wd_ref,
    gt_out, gg_out, gu_out, gd_out,
    gx, gy, gc, wg, wu, wd, xr, do, hid, dgu, drows, pm,
    t0, t1, ra0, ra1, rb0, rb1, sa0, sa1, sb0, sb1,
    wp, sib, rz, dn, dsib, drz,
    local_sem, send_sem, recv_sem,
):
    tok, width, ff, held, cap, top, nz = dims
    half = tok // 2
    hw, qw = width // 2, width // 4
    dp = lax.axis_index("dp")
    ex = lax.axis_index("expert")
    core, z = lax.rem(dp, 2), lax.div(dp, 2)
    px, py = lax.rem(ex, SIDE), lax.div(ex, SIDE)

    def near(axis, step):
        if axis == "x":
            return (dp, py * SIDE + lax.rem(px + step + SIDE, SIDE))
        if axis == "y":
            return (dp, lax.rem(py + step + SIDE, SIDE) * SIDE + px)
        if axis == "z":
            return (lax.rem(z + step + nz, nz) * 2 + core, ex)
        return (z * 2 + 1 - core, ex)

    partners = [near("x", 1), near("x", -1), near("y", 1), near("y", -1),
                near("z", 1), near("z", -1), near("core", 1)]

    count = [0]
    sent = []

    def push(src, dst, where):
        k = count[0]
        count[0] += 1
        copy = pltpu.make_async_remote_copy(
            src_ref=src, dst_ref=dst, send_sem=send_sem.at[k], recv_sem=recv_sem.at[k],
            device_id=where, device_id_type=MESH,
        )
        copy.start()
        sent.append(copy)
        return copy

    owns = [pltpu.make_async_copy(a, b, local_sem.at[i])
            for i, (a, b) in enumerate(((tok_ref, gx.at[0]), (gout_ref, gy.at[0])))]
    for own in owns:
        own.start()
    loads = [pltpu.make_async_copy(a, b, local_sem.at[2 + i])
             for i, (a, b) in enumerate(((wg_ref, wg), (wu_ref, wu), (wd_ref, wd)))]

    barrier = pltpu.get_barrier_semaphore()
    for who in partners:
        pl.semaphore_signal(barrier, inc=1, device_id=who, device_id_type=MESH)

    peers = SIDE * SIDE
    ids = lax.broadcasted_iota(jnp.int32, (peers, tok), 0) * held
    for j in range(held):
        total = jnp.zeros((peers, tok), F32)
        for k in range(top):
            total = total + jnp.where(
                routes_ref[k:k + 1, :] == ids + j, comb_ref[k:k + 1, :].astype(F32), 0.0)
        gc[0, :, j * tok:(j + 1) * tok] = total.astype(BF)

    for own in owns:
        own.wait()
    pl.semaphore_wait(barrier, len(partners))

    arrays = {"c": (gc, "x", "y"), "x": (gx, "x", "y"), "y": (gy, "y", "x")}
    coming = {}

    def slot(name, o1, o2):
        return o2 * SIDE + o1 if arrays[name][1] == "x" else o1 * SIDE + o2

    def hop(name, o1, o2, which, step, far=False):
        ref, axis = arrays[name][0], arrays[name][which]
        l1, l2 = ((o1 - step) % SIDE, o2) if which == 1 else (o1, (o2 - step) % SIDE)
        src, dst = ref.at[slot(name, o1, o2)], ref.at[slot(name, l1, l2)]
        if far and name != "c":
            at = 0 if step == 1 else half
            src, dst = src.at[pl.ds(at, half)], dst.at[pl.ds(at, half)]
        coming.setdefault((name, l1, l2), []).append(push(src, dst, near(axis, step)))

    def begin(name):
        for which in (1, 2):
            for step in (1, -1):
                hop(name, 0, 0, which, step)

    def arrive(name, *offsets):
        for o1, o2 in offsets:
            for copy in coming[(name, o1, o2)]:
                copy.wait_recv()
            which, off = (1, o1) if o2 == 0 else (2, o2)
            if off == 3:
                hop(name, o1, o2, which, 1, True)
            if off == 1 and name != "c":
                hop(name, o1, o2, which, -1, True)
            if which == 1:
                for step in (1, -1):
                    hop(name, o1, o2, 2, step)

    n1, n2, f1 = ((3, 0), (1, 0)), ((0, 3), (0, 1)), ((2, 0),)
    mid, f2, g1, g2, last = ((3, 3), (3, 1), (1, 3), (1, 1)), ((0, 2),), ((2, 3), (2, 1)), ((3, 2), (1, 2)), ((2, 2),)

    begin("c")
    begin("x")
    begin("y")
    for load in loads:
        load.start()

    lower = lax.broadcasted_iota(jnp.int32, (tok, tok), 0)
    upper = lax.broadcasted_iota(jnp.int32, (tok, tok), 1)
    before = (lower < upper).astype(BF)
    slots_in = lax.broadcasted_iota(jnp.int32, (cap, tok), 0).astype(F32)
    mine = lax.broadcasted_iota(jnp.int32, (peers, held * tok), 0) == ex

    def select(b, *which):
        for n in which:
            ox, oy = BATCHES[b][n]
            i, s = STARTS[b] + n, oy * SIDE + ox
            weight = jnp.sum(jnp.where(mine, gc[s].astype(F32), 0.0), axis=0, keepdims=True)
            named = jnp.where(weight > 0.0, 1.0, 0.0)
            taken = []
            for j in range(held):
                lane = named[:, j * tok:(j + 1) * tok]
                rank = dot_nn(jnp.broadcast_to(lane, (16, tok)).astype(BF), before)[0:1, :]
                taken.append(jnp.where((slots_in == rank) & (lane > 0.0), 1.0, 0.0))
            pick = jnp.concatenate(taken, axis=0).astype(BF)
            pm[i] = pick
            scaled = jnp.concatenate(
                [taken[j] * weight[:, j * tok:(j + 1) * tok] for j in range(held)], axis=0).astype(BF)
            rows_x = dot_nn(pick, gx[s]).astype(BF)
            rows_d = dot_nn(scaled, gy[s]).astype(BF)
            for j in range(held):
                xr[j, i * cap:(i + 1) * cap, :] = rows_x[j * cap:(j + 1) * cap]
                do[j, i * cap:(i + 1) * cap, :] = rows_d[j * cap:(j + 1) * cap]

    def hidden_part(b):
        rows = slice(STARTS[b] * cap, STARTS[b + 1] * cap)

        def expert(e, carry):
            x = xr[e, rows, :]
            gate = dot_nn(x, wg[e])
            up = dot_nn(x, wu[e])
            sg = jax.nn.sigmoid(gate)
            hid[e, rows, :] = (gate * sg * up).astype(BF)
            dgu[e, rows, 0:ff] = (up * sg * (1.0 + gate * (1.0 - sg))).astype(BF)
            dgu[e, rows, ff:2 * ff] = (gate * sg).astype(BF)
            return carry

        lax.fori_loop(0, held, expert, 0)

    def gates_part(b):
        rows = slice(STARTS[b] * cap, STARTS[b + 1] * cap)

        def expert(e, carry):
            dh = dot_nt(do[e, rows, :], wd[e])
            dgu[e, rows, 0:ff] = (dh * dgu[e, rows, 0:ff].astype(F32)).astype(BF)
            dgu[e, rows, ff:2 * ff] = (dh * dgu[e, rows, ff:2 * ff].astype(F32)).astype(BF)
            return carry

        lax.fori_loop(0, held, expert, 0)

    def rows_part(b):
        rows = slice(STARTS[b] * cap, STARTS[b + 1] * cap)

        def expert(e, carry):
            back = (dot_nt(dgu[e, rows, 0:ff], wg[e]) + dot_nt(dgu[e, rows, ff:2 * ff], wu[e])).astype(BF)
            for i in range(len(BATCHES[b])):
                drows[i, e] = back[i * cap:(i + 1) * cap]
            return carry

        lax.fori_loop(0, held, expert, 0)
        for i, (ox, oy) in enumerate(BATCHES[b]):
            part = dot_tn(pm[STARTS[b] + i], drows[i].reshape(held * cap, width)).astype(BF)
            t0[ox, oy] = part[:, 0:hw]
            t1[oy, ox] = part[:, hw:width]

    def far_send(t, ra, axis):
        return [push(t.at[2, :, pl.ds(0, half)], ra.at[0], near(axis, 1)),
                push(t.at[2, :, pl.ds(half, half)], ra.at[1], near(axis, -1))]

    def near_send(t, ra, rb, axis, copies):
        copies[0].wait_recv()
        copies[1].wait_recv()
        for i in range(SIDE):
            t[1, i, 0:half] = (t[1, i, 0:half].astype(F32) + ra[0, i].astype(F32)).astype(BF)
            t[3, i, half:tok] = (t[3, i, half:tok].astype(F32) + ra[1, i].astype(F32)).astype(BF)
        return [push(t.at[1], rb.at[0], near(axis, 1)), push(t.at[3], rb.at[1], near(axis, -1))]

    def near_sum(t, rb, copies):
        copies[0].wait_recv()
        copies[1].wait_recv()
        for i in range(SIDE):
            t[0, i] = (t[0, i].astype(F32) + rb[0, i].astype(F32) + rb[1, i].astype(F32)).astype(BF)

    def far_send2(t, sa, axis):
        return [push(t.at[0, 2, pl.ds(0, half)], sa.at[0], near(axis, 1)),
                push(t.at[0, 2, pl.ds(half, half)], sa.at[1], near(axis, -1))]

    def near_send2(t, sa, sb, axis, copies):
        copies[0].wait_recv()
        copies[1].wait_recv()
        t[0, 1, 0:half] = (t[0, 1, 0:half].astype(F32) + sa[0].astype(F32)).astype(BF)
        t[0, 3, half:tok] = (t[0, 3, half:tok].astype(F32) + sa[1].astype(F32)).astype(BF)
        return [push(t.at[0, 1], sb.at[0], near(axis, 1)), push(t.at[0, 3], sb.at[1], near(axis, -1))]

    def last_sum(t, sb, at, copies):
        copies[0].wait_recv()
        copies[1].wait_recv()
        gt_out[:, at:at + hw] = (
            t[0, 0].astype(F32) + sb[0].astype(F32) + sb[1].astype(F32)).astype(BF)

    gr, dr = width // (2 * nz), ff // (2 * nz)

    def gate_up(e):
        def piece(p, carry):
            at = pl.multiple_of(p * 4 * gr, 4 * gr)
            res = dot_tn(xr[e, :, pl.ds(at, 4 * gr)], dgu[e]).astype(BF)
            for q in range(4):
                for d in range(2):
                    wp[q % 2, e, 2 * p + q // 2, d] = res[q * gr:(q + 1) * gr, d * ff:(d + 1) * ff]
            return carry

        lax.fori_loop(0, nz // 2, piece, 0)
        return push(wp.at[1 - core, e], sib.at[e], near("core", 1))

    def down(hi):
        def expert(e, carry):
            res = dot_tn(hid[e], do[e, :, hi * hw:(hi + 1) * hw]).astype(BF)
            for q in range(2 * nz):
                for d in range(2):
                    dn[hi, q % 2, q // 2, d, e] = res[q * dr:(q + 1) * dr, d * qw:(d + 1) * qw]
            return carry

        lax.fori_loop(0, held, expert, 0)
        return push(dn.at[hi, 1 - core], dsib.at[hi], near("core", 1))

    ring = {}

    def ring_block(d, k):
        return lax.rem(z - 1 - k + 2 * nz, nz) if d == 0 else lax.rem(z + 1 + k, nz)

    def ring_step(e, k):
        for d in range(2):
            b = ring_block(d, k)
            total = wp[core, e, b, d].astype(F32) + sib[e, b, d].astype(F32)
            if k > 0:
                ring[(e, d)].wait_recv()
                total = total + rz[e, k - 1, d].astype(F32)
            total = total.astype(BF)
            if k < nz - 1:
                wp[core, e, b, d] = total
                ring[(e, d)] = push(
                    wp.at[core, e, b, d], rz.at[e, k, d], near("z", 1 if d == 0 else -1))
            else:
                out = gg_out if d == 0 else gu_out
                out[e] = total

    def down_step(hi, k):
        for d in range(2):
            b = ring_block(d, k)
            total = dn[hi, core, b, d].astype(F32) + dsib[hi, b, d].astype(F32)
            if k > 0:
                ring[("down", hi, d)].wait_recv()
                total = total + drz[hi, k - 1, d].astype(F32)
            total = total.astype(BF)
            if k < nz - 1:
                dn[hi, core, b, d] = total
                ring[("down", hi, d)] = push(
                    dn.at[hi, core, b, d], drz.at[hi, k, d], near("z", 1 if d == 0 else -1))
            else:
                at = hi * hw + d * qw
                gd_out[:, :, at:at + qw] = total

    def every(*offsets):
        for name in ("c", "x", "y"):
            arrive(name, *offsets)

    low = [None, None]
    pair = [None] * held
    at_ring = [0] * held
    at_down = [0, 0]

    def ring_next(*which):
        for e in which:
            if at_ring[e] == 0:
                pair[e].wait_recv()
            ring_step(e, at_ring[e])
            at_ring[e] += 1

    def down_next(*which):
        for hi in which:
            if at_down[hi] == 0:
                low[hi].wait_recv()
            down_step(hi, at_down[hi])
            at_down[hi] += 1

    every(*n1)
    every(*n2)
    for load in loads:
        load.wait()
    select(0, 0, 1, 2, 3, 4)
    hidden_part(0)
    gates_part(0)
    rows_part(0)
    every(*f1)
    every(*mid)
    every(*f2)
    select(1, 0, 1, 2, 3, 4, 5)
    hidden_part(1)
    gates_part(1)
    every(*g1)
    rows_part(1)
    every(*g2)
    select(2, 0, 1, 2, 3)
    every(*last)
    select(2, 4)
    hidden_part(2)
    low[0] = down(0)
    low[1] = down(1)
    gates_part(2)
    down_next(0, 1)
    pair[0] = gate_up(0)
    down_next(0, 1)
    pair[1] = gate_up(1)
    ring_next(0)
    down_next(0, 1)
    pair[2] = gate_up(2)
    ring_next(1)
    rows_part(2)
    ca0, ca1 = far_send(t0, ra0, "x"), far_send(t1, ra1, "y")
    ring_next(0)
    down_next(0, 1)
    ring_next(2, 1, 0)
    down_next(0, 1)
    ring_next(2)
    cb0 = near_send(t0, ra0, rb0, "x", ca0)
    cb1 = near_send(t1, ra1, rb1, "y", ca1)
    ring_next(1, 0)
    down_next(0, 1)
    ring_next(2, 1, 0)
    down_next(0, 1)
    near_sum(t0, rb0, cb0)
    ca0 = far_send2(t0, sa0, "y")
    near_sum(t1, rb1, cb1)
    ca1 = far_send2(t1, sa1, "x")
    ring_next(2, 1, 0)
    down_next(0, 1)
    cb0 = near_send2(t0, sa0, sb0, "y", ca0)
    cb1 = near_send2(t1, sa1, sb1, "x", ca1)
    ring_next(2, 1, 0)
    last_sum(t0, sb0, 0, cb0)
    last_sum(t1, sb1, hw, cb1)
    ring_next(2, 1, 0)
    ring_next(2, 1, 2)
    for copy in sent:
        copy.wait_send()


def hand_on(*refs):
    copies = [pltpu.make_async_copy(refs[i], refs[4 + i], refs[8].at[i]) for i in range(4)]
    for copy in copies:
        copy.start()
    for copy in copies:
        copy.wait()


COPIES = 15 + 40 + 16


def shards(tokens, grad_out, routes, combine, w_gate, w_up, w_down):
    tok, width = tokens.shape
    top = routes.shape[1]
    held, unused, ff = w_gate.shape
    peers = lax.axis_size("expert")
    nz = lax.axis_size("dp") // 2
    cap = 8 * ((tok * top * 6 // (5 * peers * held) + 7) // 8)
    dims = (tok, width, ff, held, cap, top, nz)
    rows, hw, half = peers * cap, width // 2, tok // 2
    gr, dr = width // (2 * nz), ff // (2 * nz)
    copies = COPIES + (held + 2) * (1 + 2 * (nz - 1))
    any_spec = pl.BlockSpec(memory_space=pl.ANY)
    vmem_spec = pl.BlockSpec(memory_space=pltpu.VMEM)
    flops = 16 * rows * held * width * ff
    found = pl.pallas_call(
        functools.partial(kernel, dims),
        out_shape=(
            jax.ShapeDtypeStruct((tok, width), BF),
            jax.ShapeDtypeStruct((held, width // (2 * nz), ff), BF),
            jax.ShapeDtypeStruct((held, width // (2 * nz), ff), BF),
            jax.ShapeDtypeStruct((held, ff // (2 * nz), width), BF),
        ),
        in_specs=[any_spec, any_spec, vmem_spec, vmem_spec, any_spec, any_spec, any_spec],
        out_specs=(vmem_spec,) * 4,
        scratch_shapes=[
            pltpu.VMEM((peers, tok, width), BF),
            pltpu.VMEM((peers, tok, width), BF),
            pltpu.VMEM((peers, peers, held * tok), BF),
            pltpu.VMEM((held, width, ff), BF),
            pltpu.VMEM((held, width, ff), BF),
            pltpu.VMEM((held, ff, width), BF),
            pltpu.VMEM((held, rows, width), BF),
            pltpu.VMEM((held, rows, width), BF),
            pltpu.VMEM((held, rows, ff), BF),
            pltpu.VMEM((held, rows, 2 * ff), BF),
            pltpu.VMEM((6, held, cap, width), BF),
            pltpu.VMEM((peers, held * cap, tok), BF),
            pltpu.VMEM((SIDE, SIDE, tok, hw), BF),
            pltpu.VMEM((SIDE, SIDE, tok, hw), BF),
            pltpu.VMEM((2, SIDE, half, hw), BF),
            pltpu.VMEM((2, SIDE, half, hw), BF),
            pltpu.VMEM((2, SIDE, tok, hw), BF),
            pltpu.VMEM((2, SIDE, tok, hw), BF),
            pltpu.VMEM((2, half, hw), BF),
            pltpu.VMEM((2, half, hw), BF),
            pltpu.VMEM((2, tok, hw), BF),
            pltpu.VMEM((2, tok, hw), BF),
            pltpu.VMEM((2, held, nz, 2, gr, ff), BF),
            pltpu.VMEM((held, nz, 2, gr, ff), BF),
            pltpu.VMEM((held, nz - 1, 2, gr, ff), BF),
            pltpu.VMEM((2, 2, nz, 2, held, dr, width // 4), BF),
            pltpu.VMEM((2, nz, 2, held, dr, width // 4), BF),
            pltpu.VMEM((2, nz - 1, 2, held, dr, width // 4), BF),
            pltpu.SemaphoreType.DMA((5,)),
            pltpu.SemaphoreType.DMA((copies,)),
            pltpu.SemaphoreType.DMA((copies,)),
        ],
        cost_estimate=pl.CostEstimate(
            flops=flops, bytes_accessed=12 * 1024 * 1024, transcendentals=rows * held * ff),
        compiler_params=pltpu.CompilerParams(
            collective_id=0, has_side_effects=True, vmem_limit_bytes=62 * 1024 * 1024),
    )(tokens, grad_out, routes.T, combine.T, w_gate, w_up, w_down)
    return pl.pallas_call(
        hand_on,
        out_shape=tuple(jax.ShapeDtypeStruct(a.shape, a.dtype) for a in found),
        in_specs=[any_spec] * 4,
        out_specs=(vmem_spec,) * 4,
        scratch_shapes=[pltpu.SemaphoreType.DMA((4,))],
    )(*found)


def solution(mesh):
    return jax.shard_map(
        shards,
        mesh=mesh,
        in_specs=(
            P(("dp", "expert"), None),
            P(("dp", "expert"), None),
            P(("dp", "expert"), None),
            P(("dp", "expert"), None),
            P("expert", None, None),
            P("expert", None, None),
            P("expert", None, None),
        ),
        out_specs=(
            P(("dp", "expert"), None),
            P("expert", "dp", None),
            P("expert", "dp", None),
            P("expert", "dp", None),
        ),
        check_vma=False,
    )
```

```python
import functools

import jax
import jax.numpy as jnp
from jax import lax
from jax.experimental import pallas as pl
from jax.experimental.pallas import tpu as pltpu
from jax.sharding import PartitionSpec as P

MESH = pl.DeviceIdType.MESH
BF = jnp.bfloat16
F32 = jnp.float32
SIDE = 4
BATCHES = (
    ((0, 0), (3, 0), (1, 0), (0, 3), (0, 1)),
    ((3, 3), (3, 1), (1, 3), (1, 1), (2, 0), (0, 2)),
    ((2, 3), (2, 1), (3, 2), (1, 2), (2, 2)),
)
STARTS = (0, 5, 11, 16)


def dot_nn(a, b):
    return lax.dot_general(a, b, (((1,), (0,)), ((), ())), preferred_element_type=F32)


def dot_nt(a, b):
    return lax.dot_general(a, b, (((1,), (1,)), ((), ())), preferred_element_type=F32)


def dot_tn(a, b):
    return lax.dot_general(a, b, (((0,), (0,)), ((), ())), preferred_element_type=F32)


def kernel(
    dims,
    tok_ref, gout_ref, routes_ref, comb_ref, wg_ref, wu_ref, wd_ref,
    gt_out, gg_out, gu_out, gd_out,
    gx, gy, gc, wg, wu, wd, xr, do, hid, dgu, drows, pm,
    t0, t1, ra0, ra1, rb0, rb1, sa0, sa1, sb0, sb1,
    wp, sib, rz, dn, dsib, drz,
    local_sem, send_sem, recv_sem,
):
    tok, width, ff, held, cap, top, nz = dims
    half = tok // 2
    peers = SIDE * SIDE
    hw = width // 2
    dp = lax.axis_index("dp")
    ex = lax.axis_index("expert")
    core, z = lax.rem(dp, 2), lax.div(dp, 2)
    px, py = lax.rem(ex, SIDE), lax.div(ex, SIDE)

    def near(axis, step):
        if axis == "x":
            return (dp, py * SIDE + lax.rem(px + step + SIDE, SIDE))
        if axis == "y":
            return (dp, lax.rem(py + step + SIDE, SIDE) * SIDE + px)
        if axis == "z":
            return (lax.rem(z + step + nz, nz) * 2 + core, ex)
        return (z * 2 + 1 - core, ex)

    partners = [near("x", 1), near("x", -1), near("y", 1), near("y", -1),
                near("z", 1), near("z", -1), near("core", 1)]

    count = [0]
    sent = []

    def push(src, dst, where):
        k = count[0]
        count[0] += 1
        copy = pltpu.make_async_remote_copy(
            src_ref=src, dst_ref=dst, send_sem=send_sem.at[k], recv_sem=recv_sem.at[k],
            device_id=where, device_id_type=MESH,
        )
        copy.start()
        sent.append(copy)
        return copy

    owns = [pltpu.make_async_copy(a, b, local_sem.at[i])
            for i, (a, b) in enumerate(((tok_ref, gx.at[0]), (gout_ref, gy.at[0])))]
    for own in owns:
        own.start()
    loads = [pltpu.make_async_copy(a, b, local_sem.at[2 + i])
             for i, (a, b) in enumerate(((wg_ref, wg), (wu_ref, wu), (wd_ref, wd)))]

    barrier = pltpu.get_barrier_semaphore()
    for who in partners:
        pl.semaphore_signal(barrier, inc=1, device_id=who, device_id_type=MESH)

    for own in owns:
        own.wait()
    pl.semaphore_wait(barrier, len(partners))

    arrays = {"c": (gc, "x", "y"), "x": (gx, "x", "y"), "y": (gy, "y", "x")}
    coming = {}

    def slot(name, o1, o2):
        return o2 * SIDE + o1 if arrays[name][1] == "x" else o1 * SIDE + o2

    def hop(name, o1, o2, which, step, far=False):
        ref, axis = arrays[name][0], arrays[name][which]
        l1, l2 = ((o1 - step) % SIDE, o2) if which == 1 else (o1, (o2 - step) % SIDE)
        src, dst = ref.at[slot(name, o1, o2)], ref.at[slot(name, l1, l2)]
        if far and name != "c":
            at = 0 if step == 1 else half
            src, dst = src.at[pl.ds(at, half)], dst.at[pl.ds(at, half)]
        coming.setdefault((name, l1, l2), []).append(push(src, dst, near(axis, step)))

    def begin(name):
        for which in (1, 2):
            for step in (1, -1):
                hop(name, 0, 0, which, step)

    def arrive(name, *offsets):
        for o1, o2 in offsets:
            for copy in coming[(name, o1, o2)]:
                copy.wait_recv()
            which, off = (1, o1) if o2 == 0 else (2, o2)
            if off == 3:
                hop(name, o1, o2, which, 1, True)
            if off == 1 and name != "c":
                hop(name, o1, o2, which, -1, True)
            if which == 1:
                for step in (1, -1):
                    hop(name, o1, o2, 2, step)

    n1, n2, f1 = ((3, 0), (1, 0)), ((0, 3), (0, 1)), ((2, 0),)
    mid, f2, g1, g2, last = ((3, 3), (3, 1), (1, 3), (1, 1)), ((0, 2),), ((2, 3), (2, 1)), ((3, 2), (1, 2)), ((2, 2),)

    begin("x")

    ids = lax.broadcasted_iota(jnp.int32, (peers, tok), 0) * held
    for j in range(held):
        total = jnp.zeros((peers, tok), F32)
        for k in range(top):
            total = total + jnp.where(
                routes_ref[k:k + 1, :] == ids + j, comb_ref[k:k + 1, :].astype(F32), 0.0)
        gc[0, :, j * tok:(j + 1) * tok] = total.astype(BF)

    begin("c")
    begin("y")
    for load in loads:
        load.start()

    lower = lax.broadcasted_iota(jnp.int32, (tok, tok), 0)
    upper = lax.broadcasted_iota(jnp.int32, (tok, tok), 1)
    before = (lower < upper).astype(BF)
    slots_in = lax.broadcasted_iota(jnp.int32, (cap, tok), 0).astype(F32)
    mine = lax.broadcasted_iota(jnp.int32, (peers, held * tok), 0) == ex

    def select(b, *which):
        for n in which:
            ox, oy = BATCHES[b][n]
            i, s = STARTS[b] + n, oy * SIDE + ox
            weight = jnp.sum(jnp.where(mine, gc[s].astype(F32), 0.0), axis=0, keepdims=True)
            named = jnp.where(weight > 0.0, 1.0, 0.0)
            taken = []
            for j in range(held):
                lane = named[:, j * tok:(j + 1) * tok]
                rank = dot_nn(jnp.broadcast_to(lane, (16, tok)).astype(BF), before)[0:1, :]
                taken.append(jnp.where((slots_in == rank) & (lane > 0.0), 1.0, 0.0))
            pick = jnp.concatenate(taken, axis=0).astype(BF)
            pm[i] = pick
            scaled = jnp.concatenate(
                [taken[j] * weight[:, j * tok:(j + 1) * tok] for j in range(held)], axis=0).astype(BF)
            rows_x = dot_nn(pick, gx[s]).astype(BF)
            rows_d = dot_nn(scaled, gy[s]).astype(BF)
            for j in range(held):
                xr[j, i * cap:(i + 1) * cap, :] = rows_x[j * cap:(j + 1) * cap]
                do[j, i * cap:(i + 1) * cap, :] = rows_d[j * cap:(j + 1) * cap]

    def hidden_part(b, *experts):
        rows = slice(STARTS[b] * cap, STARTS[b + 1] * cap)

        def expert(e, carry):
            x = xr[e, rows, :]
            gate = dot_nn(x, wg[e])
            up = dot_nn(x, wu[e])
            sg = jax.nn.sigmoid(gate)
            hid[e, rows, :] = (gate * sg * up).astype(BF)
            dgu[e, rows, 0:ff] = (up * sg * (1.0 + gate * (1.0 - sg))).astype(BF)
            dgu[e, rows, ff:2 * ff] = (gate * sg).astype(BF)
            return carry

        if experts:
            expert(experts[0], 0)
        else:
            lax.fori_loop(0, held, expert, 0)

    def gates_part(b, *experts):
        rows = slice(STARTS[b] * cap, STARTS[b + 1] * cap)

        def expert(e, carry):
            dh = dot_nt(do[e, rows, :], wd[e])
            dgu[e, rows, 0:ff] = (dh * dgu[e, rows, 0:ff].astype(F32)).astype(BF)
            dgu[e, rows, ff:2 * ff] = (dh * dgu[e, rows, ff:2 * ff].astype(F32)).astype(BF)
            return carry

        if experts:
            expert(experts[0], 0)
        else:
            lax.fori_loop(0, held, expert, 0)

    def rows_part(b, *experts):
        rows = slice(STARTS[b] * cap, STARTS[b + 1] * cap)

        def expert(e, carry):
            back = (dot_nt(dgu[e, rows, 0:ff], wg[e]) + dot_nt(dgu[e, rows, ff:2 * ff], wu[e])).astype(BF)
            for i in range(len(BATCHES[b])):
                drows[i, e] = back[i * cap:(i + 1) * cap]
            return carry

        if experts:
            expert(experts[0], 0)
        else:
            lax.fori_loop(0, held, expert, 0)
        if experts:
            return
        token_part(b)

    def token_part(b):
        for i, (ox, oy) in enumerate(BATCHES[b]):
            part = dot_tn(pm[STARTS[b] + i], drows[i].reshape(held * cap, width)).astype(BF)
            t0[ox, oy] = part[:, 0:hw]
            t1[oy, ox] = part[:, hw:width]

    def far_send(t, ra, axis):
        return [push(t.at[2, :, pl.ds(0, half)], ra.at[0], near(axis, 1)),
                push(t.at[2, :, pl.ds(half, half)], ra.at[1], near(axis, -1))]

    def near_send(t, ra, rb, axis, copies):
        copies[0].wait_recv()
        copies[1].wait_recv()
        for i in range(SIDE):
            t[1, i, 0:half] = (t[1, i, 0:half].astype(F32) + ra[0, i].astype(F32)).astype(BF)
            t[3, i, half:tok] = (t[3, i, half:tok].astype(F32) + ra[1, i].astype(F32)).astype(BF)
        return [push(t.at[1], rb.at[0], near(axis, 1)), push(t.at[3], rb.at[1], near(axis, -1))]

    def near_sum(t, rb, copies):
        copies[0].wait_recv()
        copies[1].wait_recv()
        for i in range(SIDE):
            t[0, i] = (t[0, i].astype(F32) + rb[0, i].astype(F32) + rb[1, i].astype(F32)).astype(BF)

    def far_send2(t, sa, axis):
        return [push(t.at[0, 2, pl.ds(0, half)], sa.at[0], near(axis, 1)),
                push(t.at[0, 2, pl.ds(half, half)], sa.at[1], near(axis, -1))]

    def near_send2(t, sa, sb, axis, copies):
        copies[0].wait_recv()
        copies[1].wait_recv()
        t[0, 1, 0:half] = (t[0, 1, 0:half].astype(F32) + sa[0].astype(F32)).astype(BF)
        t[0, 3, half:tok] = (t[0, 3, half:tok].astype(F32) + sa[1].astype(F32)).astype(BF)
        return [push(t.at[0, 1], sb.at[0], near(axis, 1)), push(t.at[0, 3], sb.at[1], near(axis, -1))]

    def last_sum(t, sb, at, copies):
        copies[0].wait_recv()
        copies[1].wait_recv()
        gt_out[:, at:at + hw] = (
            t[0, 0].astype(F32) + sb[0].astype(F32) + sb[1].astype(F32)).astype(BF)

    gr, dr = width // (2 * nz), ff // (2 * nz)

    def gate_up(e):
        def piece(p, carry):
            at = pl.multiple_of(p * 4 * gr, 4 * gr)
            res = dot_tn(xr[e, :, pl.ds(at, 4 * gr)], dgu[e]).astype(BF)
            for q in range(4):
                for d in range(2):
                    wp[q % 2, e, 2 * p + q // 2, d] = res[q * gr:(q + 1) * gr, d * ff:(d + 1) * ff]
            return carry

        lax.fori_loop(0, nz // 2, piece, 0)
        return push(wp.at[1 - core, e], sib.at[e], near("core", 1))

    def down(e):
        res = dot_tn(hid[e], do[e]).astype(BF)
        for q in range(2 * nz):
            for d in range(2):
                dn[q % 2, e, q // 2, d] = res[q * dr:(q + 1) * dr, d * hw:(d + 1) * hw]
        return push(dn.at[1 - core, e], dsib.at[e], near("core", 1))

    ring = {}

    def ring_block(d, k):
        return lax.rem(z - 1 - k + 2 * nz, nz) if d == 0 else lax.rem(z + 1 + k, nz)

    def ring_step(e, k):
        for d in range(2):
            b = ring_block(d, k)
            total = wp[core, e, b, d].astype(F32) + sib[e, b, d].astype(F32)
            if k > 0:
                ring[(e, d)].wait_recv()
                total = total + rz[e, k - 1, d].astype(F32)
            total = total.astype(BF)
            if k < nz - 1:
                wp[core, e, b, d] = total
                ring[(e, d)] = push(
                    wp.at[core, e, b, d], rz.at[e, k, d], near("z", 1 if d == 0 else -1))
            else:
                out = gg_out if d == 0 else gu_out
                out[e] = total

    def down_step(e, k):
        for d in range(2):
            b = ring_block(d, k)
            total = dn[core, e, b, d].astype(F32) + dsib[e, b, d].astype(F32)
            if k > 0:
                ring[("down", e, d)].wait_recv()
                total = total + drz[e, k - 1, d].astype(F32)
            total = total.astype(BF)
            if k < nz - 1:
                dn[core, e, b, d] = total
                ring[("down", e, d)] = push(
                    dn.at[core, e, b, d], drz.at[e, k, d], near("z", 1 if d == 0 else -1))
            else:
                gd_out[e, :, d * hw:(d + 1) * hw] = total

    def every(*offsets):
        for name in ("c", "x", "y"):
            arrive(name, *offsets)

    low = [None] * held
    pair = [None] * held
    at_ring = [0] * held
    at_down = [0] * held

    def ring_next(*which):
        for e in which:
            if at_ring[e] == 0:
                pair[e].wait_recv()
            ring_step(e, at_ring[e])
            at_ring[e] += 1

    def down_next(*which):
        for e in which:
            if at_down[e] == 0:
                low[e].wait_recv()
            down_step(e, at_down[e])
            at_down[e] += 1

    arrive("x", *n1, *n2)
    arrive("c", *n1, *n2)
    arrive("y", *n1, *n2)
    for load in loads:
        load.wait()
    select(0, 0, 1, 2, 3, 4)
    hidden_part(0)
    gates_part(0)
    rows_part(0)
    every(*f1)
    every(*mid)
    every(*f2)
    select(1, 0, 1, 2, 3, 4, 5)
    hidden_part(1)
    gates_part(1)
    every(*g1)
    rows_part(1)
    every(*g2)
    select(2, 0, 1, 2, 3)
    every(*last)
    select(2, 4)
    hidden_part(2, 0)
    low[0] = down(0)
    hidden_part(2, 1)
    low[1] = down(1)
    down_next(0)
    hidden_part(2, 2)
    low[2] = down(2)
    down_next(1, 0)
    gates_part(2, 0)
    pair[0] = gate_up(0)
    down_next(2, 1, 0)
    gates_part(2, 1)
    pair[1] = gate_up(1)
    ring_next(0)
    down_next(2, 1, 0)
    gates_part(2, 2)
    pair[2] = gate_up(2)
    ring_next(1, 0)
    down_next(2, 1, 0)
    rows_part(2, 0)
    ring_next(2)
    rows_part(2, 1)
    ring_next(1, 0)
    down_next(2, 1, 0)
    rows_part(2, 2)
    token_part(2)
    ca0, ca1 = far_send(t0, ra0, "x"), far_send(t1, ra1, "y")
    ring_next(2, 1, 0)
    down_next(2, 1, 0)
    ring_next(2, 1, 0)
    cb0 = near_send(t0, ra0, rb0, "x", ca0)
    cb1 = near_send(t1, ra1, rb1, "y", ca1)
    down_next(2, 1, 0)
    ring_next(2, 1, 0)
    down_next(2, 1)
    ring_next(2, 1)
    near_sum(t0, rb0, cb0)
    ca0 = far_send2(t0, sa0, "y")
    near_sum(t1, rb1, cb1)
    ca1 = far_send2(t1, sa1, "x")
    ring_next(0)
    down_next(2)
    ring_next(2, 1)
    cb0 = near_send2(t0, sa0, sb0, "y", ca0)
    cb1 = near_send2(t1, sa1, sb1, "x", ca1)
    ring_next(0, 2, 1)
    last_sum(t0, sb0, 0, cb0)
    last_sum(t1, sb1, hw, cb1)
    ring_next(2)
    assert at_ring == [nz] * held and at_down == [nz] * held, (at_ring, at_down)
    for copy in sent:
        copy.wait_send()


def hand_on(*refs):
    copies = [pltpu.make_async_copy(refs[i], refs[4 + i], refs[8].at[i]) for i in range(4)]
    for copy in copies:
        copy.start()
    for copy in copies:
        copy.wait()


COPIES = 15 + 40 + 16


def shards(tokens, grad_out, routes, combine, w_gate, w_up, w_down):
    tok, width = tokens.shape
    top = routes.shape[1]
    held, unused, ff = w_gate.shape
    peers = lax.axis_size("expert")
    nz = lax.axis_size("dp") // 2
    cap = 8 * ((tok * top * 6 // (5 * peers * held) + 7) // 8)
    dims = (tok, width, ff, held, cap, top, nz)
    rows, hw, half = peers * cap, width // 2, tok // 2
    gr, dr = width // (2 * nz), ff // (2 * nz)
    copies = COPIES + 2 * held * (1 + 2 * (nz - 1))
    any_spec = pl.BlockSpec(memory_space=pl.ANY)
    vmem_spec = pl.BlockSpec(memory_space=pltpu.VMEM)
    flops = 16 * rows * held * width * ff
    found = pl.pallas_call(
        functools.partial(kernel, dims),
        out_shape=(
            jax.ShapeDtypeStruct((tok, width), BF),
            jax.ShapeDtypeStruct((held, width // (2 * nz), ff), BF),
            jax.ShapeDtypeStruct((held, width // (2 * nz), ff), BF),
            jax.ShapeDtypeStruct((held, ff // (2 * nz), width), BF),
        ),
        in_specs=[any_spec, any_spec, vmem_spec, vmem_spec, any_spec, any_spec, any_spec],
        out_specs=(vmem_spec,) * 4,
        scratch_shapes=[
            pltpu.VMEM((peers, tok, width), BF),
            pltpu.VMEM((peers, tok, width), BF),
            pltpu.VMEM((peers, peers, held * tok), BF),
            pltpu.VMEM((held, width, ff), BF),
            pltpu.VMEM((held, width, ff), BF),
            pltpu.VMEM((held, ff, width), BF),
            pltpu.VMEM((held, rows, width), BF),
            pltpu.VMEM((held, rows, width), BF),
            pltpu.VMEM((held, rows, ff), BF),
            pltpu.VMEM((held, rows, 2 * ff), BF),
            pltpu.VMEM((6, held, cap, width), BF),
            pltpu.VMEM((peers, held * cap, tok), BF),
            pltpu.VMEM((SIDE, SIDE, tok, hw), BF),
            pltpu.VMEM((SIDE, SIDE, tok, hw), BF),
            pltpu.VMEM((2, SIDE, half, hw), BF),
            pltpu.VMEM((2, SIDE, half, hw), BF),
            pltpu.VMEM((2, SIDE, tok, hw), BF),
            pltpu.VMEM((2, SIDE, tok, hw), BF),
            pltpu.VMEM((2, half, hw), BF),
            pltpu.VMEM((2, half, hw), BF),
            pltpu.VMEM((2, tok, hw), BF),
            pltpu.VMEM((2, tok, hw), BF),
            pltpu.VMEM((2, held, nz, 2, gr, ff), BF),
            pltpu.VMEM((held, nz, 2, gr, ff), BF),
            pltpu.VMEM((held, nz - 1, 2, gr, ff), BF),
            pltpu.VMEM((2, held, nz, 2, dr, hw), BF),
            pltpu.VMEM((held, nz, 2, dr, hw), BF),
            pltpu.VMEM((held, nz - 1, 2, dr, hw), BF),
            pltpu.SemaphoreType.DMA((5,)),
            pltpu.SemaphoreType.DMA((copies,)),
            pltpu.SemaphoreType.DMA((copies,)),
        ],
        cost_estimate=pl.CostEstimate(
            flops=flops, bytes_accessed=12 * 1024 * 1024, transcendentals=rows * held * ff),
        compiler_params=pltpu.CompilerParams(
            collective_id=0, has_side_effects=True, vmem_limit_bytes=62 * 1024 * 1024),
    )(tokens, grad_out, routes.T, combine.T, w_gate, w_up, w_down)
    return pl.pallas_call(
        hand_on,
        out_shape=tuple(jax.ShapeDtypeStruct(a.shape, a.dtype) for a in found),
        in_specs=[any_spec] * 4,
        out_specs=(vmem_spec,) * 4,
        scratch_shapes=[pltpu.SemaphoreType.DMA((4,))],
    )(*found)


def solution(mesh):
    return jax.shard_map(
        shards,
        mesh=mesh,
        in_specs=(
            P(("dp", "expert"), None),
            P(("dp", "expert"), None),
            P(("dp", "expert"), None),
            P(("dp", "expert"), None),
            P("expert", None, None),
            P("expert", None, None),
            P("expert", None, None),
        ),
        out_specs=(
            P(("dp", "expert"), None),
            P("expert", "dp", None),
            P("expert", "dp", None),
            P("expert", "dp", None),
        ),
        check_vma=False,
    )
```

```python
import functools

import jax
import jax.numpy as jnp
from jax import lax
from jax.experimental import pallas as pl
from jax.experimental.pallas import tpu as pltpu
from jax.sharding import PartitionSpec as P

MESH = pl.DeviceIdType.MESH
BF = jnp.bfloat16
F32 = jnp.float32
SIDE = 4
BATCHES = (
    ((0, 0), (3, 0), (1, 0), (0, 3), (0, 1)),
    ((3, 3), (3, 1), (1, 3), (1, 1), (2, 0), (0, 2)),
    ((2, 3), (2, 1), (3, 2), (1, 2), (2, 2)),
)
STARTS = (0, 5, 11, 16)


def dot_nn(a, b):
    return lax.dot_general(a, b, (((1,), (0,)), ((), ())), preferred_element_type=F32)


def dot_nt(a, b):
    return lax.dot_general(a, b, (((1,), (1,)), ((), ())), preferred_element_type=F32)


def dot_tn(a, b):
    return lax.dot_general(a, b, (((0,), (0,)), ((), ())), preferred_element_type=F32)


def kernel(
    dims,
    tok_ref, gout_ref, routes_ref, comb_ref, wg_ref, wu_ref, wd_ref,
    gt_out, gg_out, gu_out, gd_out,
    gx, gy, gc, wg, wu, wd, xr, do, hid, dgu, drows, pm,
    t0, t1, ra0, ra1, rb0, rb1, sa0, sa1, sb0, sb1,
    wp, sib, rz, dn, dsib, drz,
    local_sem, send_sem, recv_sem,
):
    tok, width, ff, held, cap, top, nz = dims
    half = tok // 2
    peers = SIDE * SIDE
    hw = width // 2
    dp = lax.axis_index("dp")
    ex = lax.axis_index("expert")
    core, z = lax.rem(dp, 2), lax.div(dp, 2)
    px, py = lax.rem(ex, SIDE), lax.div(ex, SIDE)

    def near(axis, step):
        if axis == "x":
            return (dp, py * SIDE + lax.rem(px + step + SIDE, SIDE))
        if axis == "y":
            return (dp, lax.rem(py + step + SIDE, SIDE) * SIDE + px)
        if axis == "z":
            return (lax.rem(z + step + nz, nz) * 2 + core, ex)
        return (z * 2 + 1 - core, ex)

    partners = [near("x", 1), near("x", -1), near("y", 1), near("y", -1),
                near("z", 1), near("z", -1), near("core", 1)]

    count = [0]
    sent = []

    def push(src, dst, where):
        k = count[0]
        count[0] += 1
        copy = pltpu.make_async_remote_copy(
            src_ref=src, dst_ref=dst, send_sem=send_sem.at[k], recv_sem=recv_sem.at[k],
            device_id=where, device_id_type=MESH,
        )
        copy.start()
        sent.append(copy)
        return copy

    owns = [pltpu.make_async_copy(a, b, local_sem.at[i])
            for i, (a, b) in enumerate(((tok_ref, gx.at[0]), (gout_ref, gy.at[0])))]
    for own in owns:
        own.start()
    loads = [pltpu.make_async_copy(a, b, local_sem.at[2 + i])
             for i, (a, b) in enumerate(((wg_ref, wg), (wu_ref, wu), (wd_ref, wd)))]

    barrier = pltpu.get_barrier_semaphore()
    for who in partners:
        pl.semaphore_signal(barrier, inc=1, device_id=who, device_id_type=MESH)

    owns[0].wait()
    pl.semaphore_wait(barrier, len(partners))

    arrays = {"c": (gc, "x", "y"), "x": (gx, "x", "y"), "y": (gy, "y", "x")}
    coming = {}

    def slot(name, o1, o2):
        return o2 * SIDE + o1 if arrays[name][1] == "x" else o1 * SIDE + o2

    def hop(name, o1, o2, which, step, far=False):
        ref, axis = arrays[name][0], arrays[name][which]
        l1, l2 = ((o1 - step) % SIDE, o2) if which == 1 else (o1, (o2 - step) % SIDE)
        src, dst = ref.at[slot(name, o1, o2)], ref.at[slot(name, l1, l2)]
        if far and name != "c":
            at = 0 if step == 1 else half
            src, dst = src.at[pl.ds(at, half)], dst.at[pl.ds(at, half)]
        coming.setdefault((name, l1, l2), []).append(push(src, dst, near(axis, step)))

    def begin(name):
        for which in (1, 2):
            for step in (1, -1):
                hop(name, 0, 0, which, step)

    def arrive(name, *offsets):
        for o1, o2 in offsets:
            for copy in coming[(name, o1, o2)]:
                copy.wait_recv()
            which, off = (1, o1) if o2 == 0 else (2, o2)
            if off == 3:
                hop(name, o1, o2, which, 1, True)
            if off == 1 and name != "c":
                hop(name, o1, o2, which, -1, True)
            if which == 1:
                for step in (1, -1):
                    hop(name, o1, o2, 2, step)

    n1, n2, f1 = ((3, 0), (1, 0)), ((0, 3), (0, 1)), ((2, 0),)
    mid, f2, g1, g2, last = ((3, 3), (3, 1), (1, 3), (1, 1)), ((0, 2),), ((2, 3), (2, 1)), ((3, 2), (1, 2)), ((2, 2),)

    begin("x")

    ids = lax.broadcasted_iota(jnp.int32, (peers, tok), 0) * held
    for j in range(held):
        total = jnp.zeros((peers, tok), F32)
        for k in range(top):
            total = total + jnp.where(
                routes_ref[k:k + 1, :] == ids + j, comb_ref[k:k + 1, :].astype(F32), 0.0)
        gc[0, :, j * tok:(j + 1) * tok] = total.astype(BF)

    begin("c")
    owns[1].wait()
    begin("y")
    for load in loads:
        load.start()

    lower = lax.broadcasted_iota(jnp.int32, (tok, tok), 0)
    upper = lax.broadcasted_iota(jnp.int32, (tok, tok), 1)
    before = (lower < upper).astype(BF)
    slots_in = lax.broadcasted_iota(jnp.int32, (cap, tok), 0).astype(F32)
    mine = lax.broadcasted_iota(jnp.int32, (peers, held * tok), 0) == ex

    def select(b, *which):
        for n in which:
            ox, oy = BATCHES[b][n]
            i, s = STARTS[b] + n, oy * SIDE + ox
            weight = jnp.sum(jnp.where(mine, gc[s].astype(F32), 0.0), axis=0, keepdims=True)
            named = jnp.where(weight > 0.0, 1.0, 0.0)
            taken = []
            for j in range(held):
                lane = named[:, j * tok:(j + 1) * tok]
                rank = dot_nn(jnp.broadcast_to(lane, (16, tok)).astype(BF), before)[0:1, :]
                taken.append(jnp.where((slots_in == rank) & (lane > 0.0), 1.0, 0.0))
            pick = jnp.concatenate(taken, axis=0).astype(BF)
            pm[i] = pick
            scaled = jnp.concatenate(
                [taken[j] * weight[:, j * tok:(j + 1) * tok] for j in range(held)], axis=0).astype(BF)
            rows_x = dot_nn(pick, gx[s]).astype(BF)
            rows_d = dot_nn(scaled, gy[s]).astype(BF)
            for j in range(held):
                xr[j, i * cap:(i + 1) * cap, :] = rows_x[j * cap:(j + 1) * cap]
                do[j, i * cap:(i + 1) * cap, :] = rows_d[j * cap:(j + 1) * cap]

    def hidden_part(b, *experts):
        rows = slice(STARTS[b] * cap, STARTS[b + 1] * cap)

        def expert(e, carry):
            x = xr[e, rows, :]
            gate = dot_nn(x, wg[e])
            up = dot_nn(x, wu[e])
            sg = jax.nn.sigmoid(gate)
            hid[e, rows, :] = (gate * sg * up).astype(BF)
            dgu[e, rows, 0:ff] = (up * sg * (1.0 + gate * (1.0 - sg))).astype(BF)
            dgu[e, rows, ff:2 * ff] = (gate * sg).astype(BF)
            return carry

        if experts:
            expert(experts[0], 0)
        else:
            lax.fori_loop(0, held, expert, 0)

    def gates_part(b, *experts):
        rows = slice(STARTS[b] * cap, STARTS[b + 1] * cap)

        def expert(e, carry):
            dh = dot_nt(do[e, rows, :], wd[e])
            dgu[e, rows, 0:ff] = (dh * dgu[e, rows, 0:ff].astype(F32)).astype(BF)
            dgu[e, rows, ff:2 * ff] = (dh * dgu[e, rows, ff:2 * ff].astype(F32)).astype(BF)
            return carry

        if experts:
            expert(experts[0], 0)
        else:
            lax.fori_loop(0, held, expert, 0)

    def rows_part(b, *experts):
        rows = slice(STARTS[b] * cap, STARTS[b + 1] * cap)

        def expert(e, carry):
            back = (dot_nt(dgu[e, rows, 0:ff], wg[e]) + dot_nt(dgu[e, rows, ff:2 * ff], wu[e])).astype(BF)
            for i in range(len(BATCHES[b])):
                drows[i, e] = back[i * cap:(i + 1) * cap]
            return carry

        if experts:
            expert(experts[0], 0)
        else:
            lax.fori_loop(0, held, expert, 0)
        if experts:
            return
        token_part(b)

    def token_part(b):
        for i, (ox, oy) in enumerate(BATCHES[b]):
            part = dot_tn(pm[STARTS[b] + i], drows[i].reshape(held * cap, width)).astype(BF)
            t0[ox, oy] = part[:, 0:hw]
            t1[oy, ox] = part[:, hw:width]

    def far_send(t, ra, axis):
        return [push(t.at[2, :, pl.ds(0, half)], ra.at[0], near(axis, 1)),
                push(t.at[2, :, pl.ds(half, half)], ra.at[1], near(axis, -1))]

    def near_send(t, ra, rb, axis, copies):
        copies[0].wait_recv()
        copies[1].wait_recv()
        for i in range(SIDE):
            t[1, i, 0:half] = (t[1, i, 0:half].astype(F32) + ra[0, i].astype(F32)).astype(BF)
            t[3, i, half:tok] = (t[3, i, half:tok].astype(F32) + ra[1, i].astype(F32)).astype(BF)
        return [push(t.at[1], rb.at[0], near(axis, 1)), push(t.at[3], rb.at[1], near(axis, -1))]

    def near_sum(t, rb, copies):
        copies[0].wait_recv()
        copies[1].wait_recv()
        for i in range(SIDE):
            t[0, i] = (t[0, i].astype(F32) + rb[0, i].astype(F32) + rb[1, i].astype(F32)).astype(BF)

    def far_send2(t, sa, axis):
        return [push(t.at[0, 2, pl.ds(0, half)], sa.at[0], near(axis, 1)),
                push(t.at[0, 2, pl.ds(half, half)], sa.at[1], near(axis, -1))]

    def near_send2(t, sa, sb, axis, copies):
        copies[0].wait_recv()
        copies[1].wait_recv()
        t[0, 1, 0:half] = (t[0, 1, 0:half].astype(F32) + sa[0].astype(F32)).astype(BF)
        t[0, 3, half:tok] = (t[0, 3, half:tok].astype(F32) + sa[1].astype(F32)).astype(BF)
        return [push(t.at[0, 1], sb.at[0], near(axis, 1)), push(t.at[0, 3], sb.at[1], near(axis, -1))]

    def last_sum(t, sb, at, copies):
        copies[0].wait_recv()
        copies[1].wait_recv()
        gt_out[:, at:at + hw] = (
            t[0, 0].astype(F32) + sb[0].astype(F32) + sb[1].astype(F32)).astype(BF)

    gr, dr = width // (2 * nz), ff // (2 * nz)

    def gate_up(e):
        def piece(p, carry):
            at = pl.multiple_of(p * 4 * gr, 4 * gr)
            res = dot_tn(xr[e, :, pl.ds(at, 4 * gr)], dgu[e]).astype(BF)
            for q in range(4):
                for d in range(2):
                    wp[q % 2, e, 2 * p + q // 2, d] = res[q * gr:(q + 1) * gr, d * ff:(d + 1) * ff]
            return carry

        lax.fori_loop(0, nz // 2, piece, 0)
        return push(wp.at[1 - core, e], sib.at[e], near("core", 1))

    def down(e):
        res = dot_tn(hid[e], do[e]).astype(BF)
        for q in range(2 * nz):
            for d in range(2):
                dn[q % 2, e, q // 2, d] = res[q * dr:(q + 1) * dr, d * hw:(d + 1) * hw]
        return push(dn.at[1 - core, e], dsib.at[e], near("core", 1))

    ring = {}

    def ring_block(d, k):
        return lax.rem(z - 1 - k + 2 * nz, nz) if d == 0 else lax.rem(z + 1 + k, nz)

    def ring_step(e, k):
        for d in range(2):
            b = ring_block(d, k)
            total = wp[core, e, b, d].astype(F32) + sib[e, b, d].astype(F32)
            if k > 0:
                ring[(e, d)].wait_recv()
                total = total + rz[e, k - 1, d].astype(F32)
            total = total.astype(BF)
            if k < nz - 1:
                wp[core, e, b, d] = total
                ring[(e, d)] = push(
                    wp.at[core, e, b, d], rz.at[e, k, d], near("z", 1 if d == 0 else -1))
            else:
                out = gg_out if d == 0 else gu_out
                out[e] = total

    def down_step(e, k):
        for d in range(2):
            b = ring_block(d, k)
            total = dn[core, e, b, d].astype(F32) + dsib[e, b, d].astype(F32)
            if k > 0:
                ring[("down", e, d)].wait_recv()
                total = total + drz[e, k - 1, d].astype(F32)
            total = total.astype(BF)
            if k < nz - 1:
                dn[core, e, b, d] = total
                ring[("down", e, d)] = push(
                    dn.at[core, e, b, d], drz.at[e, k, d], near("z", 1 if d == 0 else -1))
            else:
                gd_out[e, :, d * hw:(d + 1) * hw] = total

    def every(*offsets):
        for name in ("c", "x", "y"):
            arrive(name, *offsets)

    low = [None] * held
    pair = [None] * held
    at_ring = [0] * held
    at_down = [0] * held

    def ring_next(*which):
        for e in which:
            if at_ring[e] == 0:
                pair[e].wait_recv()
            ring_step(e, at_ring[e])
            at_ring[e] += 1

    def down_next(*which):
        for e in which:
            if at_down[e] == 0:
                low[e].wait_recv()
            down_step(e, at_down[e])
            at_down[e] += 1

    arrive("x", *n1, *n2)
    arrive("c", *n1, *n2)
    arrive("y", *n1, *n2)
    for load in loads:
        load.wait()
    select(0, 0, 1, 2, 3, 4)
    hidden_part(0)
    gates_part(0)
    rows_part(0)
    every(*f1)
    every(*mid)
    every(*f2)
    select(1, 0, 1, 2, 3, 4, 5)
    hidden_part(1)
    gates_part(1)
    every(*g1)
    rows_part(1)
    every(*g2)
    select(2, 0, 1, 2, 3)
    every(*last)
    select(2, 4)
    hidden_part(2, 0)
    low[0] = down(0)
    hidden_part(2, 1)
    low[1] = down(1)
    down_next(0)
    hidden_part(2, 2)
    low[2] = down(2)
    down_next(1, 0)
    gates_part(2, 0)
    pair[0] = gate_up(0)
    down_next(2, 1, 0)
    gates_part(2, 1)
    pair[1] = gate_up(1)
    ring_next(0)
    down_next(2, 1, 0)
    gates_part(2, 2)
    pair[2] = gate_up(2)
    ring_next(1, 0)
    down_next(2, 1, 0)
    rows_part(2, 0)
    ring_next(2)
    rows_part(2, 1)
    ring_next(1, 0)
    down_next(2, 1, 0)
    rows_part(2, 2)
    token_part(2)
    ca0, ca1 = far_send(t0, ra0, "x"), far_send(t1, ra1, "y")
    ring_next(2, 1, 0)
    down_next(2, 1, 0)
    ring_next(2, 1, 0)
    cb0 = near_send(t0, ra0, rb0, "x", ca0)
    cb1 = near_send(t1, ra1, rb1, "y", ca1)
    down_next(2, 1, 0)
    ring_next(2, 1, 0)
    down_next(2, 1)
    ring_next(2, 1)
    near_sum(t0, rb0, cb0)
    ca0 = far_send2(t0, sa0, "y")
    near_sum(t1, rb1, cb1)
    ca1 = far_send2(t1, sa1, "x")
    ring_next(0)
    down_next(2)
    ring_next(2, 1)
    cb0 = near_send2(t0, sa0, sb0, "y", ca0)
    cb1 = near_send2(t1, sa1, sb1, "x", ca1)
    ring_next(0, 2, 1)
    last_sum(t0, sb0, 0, cb0)
    last_sum(t1, sb1, hw, cb1)
    ring_next(2)
    assert at_ring == [nz] * held and at_down == [nz] * held, (at_ring, at_down)
    for copy in sent:
        copy.wait_send()


def hand_on(*refs):
    copies = [pltpu.make_async_copy(refs[i], refs[4 + i], refs[8].at[i]) for i in range(4)]
    for copy in copies:
        copy.start()
    for copy in copies:
        copy.wait()


COPIES = 15 + 40 + 16


def shards(tokens, grad_out, routes, combine, w_gate, w_up, w_down):
    tok, width = tokens.shape
    top = routes.shape[1]
    held, unused, ff = w_gate.shape
    peers = lax.axis_size("expert")
    nz = lax.axis_size("dp") // 2
    cap = 8 * ((tok * top * 6 // (5 * peers * held) + 7) // 8)
    dims = (tok, width, ff, held, cap, top, nz)
    rows, hw, half = peers * cap, width // 2, tok // 2
    gr, dr = width // (2 * nz), ff // (2 * nz)
    copies = COPIES + 2 * held * (1 + 2 * (nz - 1))
    any_spec = pl.BlockSpec(memory_space=pl.ANY)
    vmem_spec = pl.BlockSpec(memory_space=pltpu.VMEM)
    flops = 16 * rows * held * width * ff
    found = pl.pallas_call(
        functools.partial(kernel, dims),
        out_shape=(
            jax.ShapeDtypeStruct((tok, width), BF),
            jax.ShapeDtypeStruct((held, width // (2 * nz), ff), BF),
            jax.ShapeDtypeStruct((held, width // (2 * nz), ff), BF),
            jax.ShapeDtypeStruct((held, ff // (2 * nz), width), BF),
        ),
        in_specs=[any_spec, any_spec, vmem_spec, vmem_spec, any_spec, any_spec, any_spec],
        out_specs=(vmem_spec,) * 4,
        scratch_shapes=[
            pltpu.VMEM((peers, tok, width), BF),
            pltpu.VMEM((peers, tok, width), BF),
            pltpu.VMEM((peers, peers, held * tok), BF),
            pltpu.VMEM((held, width, ff), BF),
            pltpu.VMEM((held, width, ff), BF),
            pltpu.VMEM((held, ff, width), BF),
            pltpu.VMEM((held, rows, width), BF),
            pltpu.VMEM((held, rows, width), BF),
            pltpu.VMEM((held, rows, ff), BF),
            pltpu.VMEM((held, rows, 2 * ff), BF),
            pltpu.VMEM((6, held, cap, width), BF),
            pltpu.VMEM((peers, held * cap, tok), BF),
            pltpu.VMEM((SIDE, SIDE, tok, hw), BF),
            pltpu.VMEM((SIDE, SIDE, tok, hw), BF),
            pltpu.VMEM((2, SIDE, half, hw), BF),
            pltpu.VMEM((2, SIDE, half, hw), BF),
            pltpu.VMEM((2, SIDE, tok, hw), BF),
            pltpu.VMEM((2, SIDE, tok, hw), BF),
            pltpu.VMEM((2, half, hw), BF),
            pltpu.VMEM((2, half, hw), BF),
            pltpu.VMEM((2, tok, hw), BF),
            pltpu.VMEM((2, tok, hw), BF),
            pltpu.VMEM((2, held, nz, 2, gr, ff), BF),
            pltpu.VMEM((held, nz, 2, gr, ff), BF),
            pltpu.VMEM((held, nz - 1, 2, gr, ff), BF),
            pltpu.VMEM((2, held, nz, 2, dr, hw), BF),
            pltpu.VMEM((held, nz, 2, dr, hw), BF),
            pltpu.VMEM((held, nz - 1, 2, dr, hw), BF),
            pltpu.SemaphoreType.DMA((5,)),
            pltpu.SemaphoreType.DMA((copies,)),
            pltpu.SemaphoreType.DMA((copies,)),
        ],
        cost_estimate=pl.CostEstimate(
            flops=flops, bytes_accessed=12 * 1024 * 1024, transcendentals=rows * held * ff),
        compiler_params=pltpu.CompilerParams(
            collective_id=0, has_side_effects=True, vmem_limit_bytes=62 * 1024 * 1024),
    )(tokens, grad_out, routes.T, combine.T, w_gate, w_up, w_down)
    return pl.pallas_call(
        hand_on,
        out_shape=tuple(jax.ShapeDtypeStruct(a.shape, a.dtype) for a in found),
        in_specs=[any_spec] * 4,
        out_specs=(vmem_spec,) * 4,
        scratch_shapes=[pltpu.SemaphoreType.DMA((4,))],
    )(*found)


def solution(mesh):
    return jax.shard_map(
        shards,
        mesh=mesh,
        in_specs=(
            P(("dp", "expert"), None),
            P(("dp", "expert"), None),
            P(("dp", "expert"), None),
            P(("dp", "expert"), None),
            P("expert", None, None),
            P("expert", None, None),
            P("expert", None, None),
        ),
        out_specs=(
            P(("dp", "expert"), None),
            P("expert", "dp", None),
            P("expert", "dp", None),
            P("expert", "dp", None),
        ),
        check_vma=False,
    )
```
